256 devices in a mesh: section: 2 (over core), expert: 128 (over x, y, z).
Axes of the slice: x: 4, y: 4, z: 8, core: 2. Of those that a mesh axis runs over, the one named last changes fastest.
Arguments:
- hidden: bfloat16 [2, 16384, 2048], P('section', 'expert'), may hold values from -6 to 6
- routes: int32 [2, 16384, 2], P('section', 'expert'), may hold values from 0 to 127, all different within a row; in each aligned block of 128 rows (0 to 127, 128 to 255, ..., all dimensions but the last counted through in order) at most 4 rows name the same one
- gates: float32 [2, 16384, 2], P('section', 'expert'), may hold values from 0.2 to 1
- lengths: int32 [2, 128], P('section', 'expert'), may hold values from 64 to 128, as said below
- w_in: bfloat16 [2, 2048, 131072], P('section', None, 'expert'), may hold values from -0.125 to 0.125
- w_out: bfloat16 [2, 131072, 2048], P('section', 'expert'), may hold values from -0.0625 to 0.0625
- incoming: bfloat16 [2, 16384, 2048], P(None, 'expert', 'section'), may hold values from -6 to 6
Outputs:
- outputs: bfloat16 [2, 16384, 2048], P('section', 'expert')
- hidden_grad: bfloat16 [2, 16384, 2048], P('section', 'expert')
- gate_grad: float32 [2, 16384, 2], P('section', 'expert')
The draws below stay inside these ranges and needn't reach their ends.
Inputs may be any that keep to these rules, and one draw needn't show every extreme that they name: `routes`: each row names two different experts. Among the rows of one sentence no expert is named more than 4 times, a bound that some block reaches. `lengths`: each layer has a sentence of exactly 128 tokens.
All inputs are finite; a program needn't handle non-finite values.
Results may differ from the reference program's by a relative error of at most 0.013.
Values may be sent and summed in bfloat16 or wider, within the bound.
No kernel may reach another device: no remote copies, remote signals or barrier semaphores. Data moves between devices by JAX's collectives and lax.ppermute only.
A program may use at most 64 MiB of HBM per device.

```python
import math
import jax
import jax.numpy as jnp
import numpy as np
from jax import lax

D = 2048
FF = 8192
EXPERTS = 128
SPLIT = 8
TOK_DEV = 128
CAP = 4
LIVE = 16
FF_DEV = 1024
TOKENS = 16384
SENTS = 128
N_EXPERT = 128


def draw_lengths(key, part):
    key = jax.random.fold_in(key, 7)
    key_lengths, key_full = jax.random.split(key)
    drawn = jax.random.randint(key_lengths, (2, SENTS), TOK_DEV // 2, TOK_DEV + 1)
    longest = jax.random.randint(key_full, (2,), 0, SENTS)
    columns = jnp.arange(SENTS)[None, :]
    return jnp.where(columns == longest[:, None], TOK_DEV, drawn).astype(jnp.int32)


def level_of(own_key, extent, cuts, smallest, largest):
    level = 1.0
    for position, blocks in cuts:
        draws = jax.random.uniform(jax.random.fold_in(jax.random.fold_in(own_key, 6), position), (blocks,), jnp.float32, smallest / len(cuts), largest / len(cuts))
        level = level * jnp.repeat(jnp.exp(draws), extent[position] // blocks).reshape((-1,) + (1,) * (len(extent) - 1 - position))
    return level


def shared_out(own_key, own, number, rows, amount, top, most, slope):
    sequence = jax.random.permutation(own_key, amount)
    crowded, usual = load_shares(amount, rows * top, most, slope, True), load_shares(amount, rows * top, most, slope, False)
    places = jnp.arange(amount)

    def named(tallies, offset_by):
        used = int((tallies > 0).sum())
        fixed = max(1, used // 4)
        shifted = fixed + (places - fixed + offset_by * (used - fixed)) % max(1, amount - fixed)
        return jnp.zeros((amount,), jnp.int32).at[sequence[jnp.where(places < fixed, places, shifted)]].set(jnp.asarray(tallies, jnp.int32))

    tallies = jnp.where(number % 4 == 0, named(crowded, number // 4), named(usual, number - number // 4 - 1))
    mixed = jax.random.permutation(jax.random.fold_in(own, 3), amount)
    donor, receiver = mixed[0:amount // 2 * 2:2], mixed[1:amount // 2 * 2:2]
    margin = jnp.minimum(tallies[donor] - 1, most - tallies[receiver]) // 2
    margin = jnp.where((donor == sequence[0]) | (receiver == sequence[0]) | (tallies[receiver] == 0), 0, jnp.maximum(margin, 0))
    shifted = jax.random.randint(jax.random.fold_in(own, 4), (amount // 2,), 0, 1 << 20) % (margin + 1)
    tallies = tallies.at[donor].add(-shifted).at[receiver].add(shifted)
    members = jnp.searchsorted(jnp.cumsum(tallies), jnp.arange(rows * top), side="right").astype(jnp.int32)
    table = members.reshape(top, rows).T
    table = table[jax.random.permutation(jax.random.fold_in(own, 1), rows)]
    offset_by = jax.random.randint(jax.random.fold_in(own, 2), (rows, 1), 0, top)
    return jnp.take_along_axis(table, (jnp.arange(top)[None, :] + offset_by) % top, axis=1)


def load_shares(amount, total, most, lean, full):
    weights = [(1 << 20) // math.isqrt(standing ** lean) + 1 for standing in range(1, amount + 1)]
    largest = most if full else min(most, max(-(-total // amount), total * weights[0] // sum(weights)))
    least = 1 if total - largest >= amount - 1 else 0
    given, rest = [largest] + [least] * (amount - 1), total - largest - least * (amount - 1)
    while rest > 0:
        free = [i for i in range(1, amount) if given[i] < largest] or [i for i in range(1, amount) if given[i] < most]
        pool, budget = sum([weights[i] for i in free]), rest
        for i in free:
            addition = min(most - given[i], max(1, budget * weights[i] // pool), rest)
            given[i] = given[i] + addition
            rest = rest - addition
    return np.array(given)


def centred(rng, shape, width, most, pieces=(), held_as=jnp.bfloat16):
    values = jax.random.normal(rng, shape, jnp.float32) * width
    if len(pieces) > 0:
        values = level_of(rng, shape, pieces, -0.22, 0.18) * values
    return jnp.clip(values, min=-most, max=most).astype(held_as)


def setup_inputs(seed: int = 0) -> dict:
    streams_of = jax.random.split(jax.random.key(seed), 8)
    hidden = centred(streams_of[0], (2, TOKENS, D), 1.0, 6.0, ((0, 2), (1, 128)))
    routes_keys = jax.random.split(jax.random.fold_in(streams_of[1], 1), 2 * TOKENS // TOK_DEV)
    routes_turns = jax.random.permutation(jax.random.fold_in(streams_of[1], 3), 2 * TOKENS // TOK_DEV)
    routes = jax.vmap(lambda own, number: shared_out(jax.random.fold_in(streams_of[1], 2), own, number, TOK_DEV, EXPERTS, 2, CAP, 2))(routes_keys, routes_turns).reshape((2, TOKENS, 2))
    gates = jnp.clip(0.2 + 0.8 * jax.random.uniform(streams_of[2], (2, TOKENS, 2), jnp.float32) ** level_of(streams_of[2], (2, TOKENS, 2), ((0, 2), (1, 128)), -0.2, 0.2), 0.2, 1.0)
    lengths = draw_lengths(jax.random.fold_in(streams_of[7], 71), 0)
    w_in = centred(streams_of[4], (2, D, LIVE * FF), D ** -0.5, 0.125, ((0, 2), (2, 128)))
    w_out = centred(streams_of[5], (2, LIVE * FF, D), FF ** -0.5, 0.0625, ((0, 2), (1, 128)))
    incoming = centred(streams_of[6], (2, TOKENS, D), 1.0, 6.0, ((1, 128), (2, 2)))
    return {"hidden": hidden, "routes": routes, "gates": gates, "lengths": lengths, "w_in": w_in, "w_out": w_out, "incoming": incoming}


EPS = 1e-05

def normalize(values):
    center = values - lax.optimization_barrier(jnp.mean(values, axis=-1, keepdims=True))
    scale = lax.rsqrt(lax.optimization_barrier(jnp.mean(center * center, axis=-1, keepdims=True)) + EPS)
    return (center * scale, scale)

def norm_back(normed, scale, upstream):
    first = lax.optimization_barrier(jnp.mean(upstream, axis=-1, keepdims=True))
    second = lax.optimization_barrier(jnp.mean(upstream * normed, axis=-1, keepdims=True))
    return scale * (upstream - first - normed * second)

def one_layer(hidden, routes, gates, lengths, w_in, w_out, incoming, layer):
    wave_size = N_EXPERT // SPLIT
    total = wave_size * N_EXPERT * CAP
    source = hidden.astype(jnp.float32)
    token_pos = jnp.arange(TOKENS, dtype=jnp.int32) % TOK_DEV
    sentence = jnp.arange(TOKENS, dtype=jnp.int32) // TOK_DEV
    alive = token_pos < lengths[sentence]
    in_wave = alive[:, None] & (routes < wave_size)
    expert_flat = routes.reshape(N_EXPERT, TOK_DEV * 2)
    wave_flat = in_wave.reshape(N_EXPERT, TOK_DEV * 2)
    onehot = ((expert_flat[:, :, None] == jnp.arange(wave_size, dtype=jnp.int32)[None, None, :]) & wave_flat[:, :, None]).astype(jnp.int32)
    rank = lax.optimization_barrier(jnp.sum((jnp.cumsum(onehot, axis=1) - onehot) * onehot, axis=-1)).astype(jnp.int32)
    senders = jnp.arange(N_EXPERT, dtype=jnp.int32)[:, None]
    slot_index = ((expert_flat * N_EXPERT + senders) * CAP + rank).astype(jnp.int32)
    slot_index = jnp.where(wave_flat, slot_index, total).reshape(-1)
    safe_index = jnp.where(wave_flat.reshape(-1), slot_index, 0)
    wave_mask = wave_flat.reshape(-1, 1).astype(jnp.float32)
    normed, scale = normalize(source)
    normed_bf = normed.astype(jnp.bfloat16)
    repeated = jnp.repeat(normed_bf, 2, axis=0)
    in_buf = jnp.zeros((total, D), jnp.bfloat16).at[slot_index].set(repeated, mode='drop')
    in_buf = in_buf.reshape(wave_size, N_EXPERT * CAP, D)

    def expert_forward(expert):
        rows = in_buf[expert]
        summed = jnp.zeros((N_EXPERT * CAP, D), jnp.float32)
        for block in range(SPLIT):
            start = ((expert * SPLIT + block) * FF_DEV).astype(jnp.int32)
            w_first = lax.dynamic_slice_in_dim(w_in, start, FF_DEV, 1)
            w_second = lax.dynamic_slice_in_dim(w_out, start, FF_DEV, 0)
            act = jnp.maximum(jnp.dot(rows, w_first, preferred_element_type=jnp.float32), 0.0).astype(jnp.bfloat16)
            part = jnp.dot(act, w_second, preferred_element_type=jnp.float32).astype(jnp.bfloat16)
            summed = summed + part.astype(jnp.float32)
        return summed
    expert_out = lax.map(expert_forward, jnp.arange(wave_size, dtype=jnp.int32)).reshape(total, D)
    y_copy = (expert_out[safe_index] * wave_mask).reshape(TOKENS, 2, D)
    mixed = source + gates[:, 0:1] * y_copy[:, 0] + gates[:, 1:2] * y_copy[:, 1]
    layer_out = mixed.astype(jnp.bfloat16)
    cotangent = incoming.astype(jnp.float32) * alive[:, None].astype(jnp.float32)
    if layer == 0:
        out_hat, out_scale = normalize(layer_out.astype(jnp.float32))
        result = out_hat.astype(jnp.bfloat16)
        upstream = norm_back(out_hat, out_scale, cotangent).astype(jnp.bfloat16)
    else:
        result = layer_out
        upstream = cotangent.astype(jnp.bfloat16)
    upstream32 = upstream.astype(jnp.float32)
    gate_grad = lax.optimization_barrier(jnp.sum(upstream32[:, None, :] * y_copy, axis=-1))
    scaled = (gates[:, :, None] * upstream32[:, None, :]).astype(jnp.bfloat16).reshape(TOKENS * 2, D)
    grad_buf = jnp.zeros((total, D), jnp.bfloat16).at[slot_index].set(scaled, mode='drop')
    grad_buf = grad_buf.reshape(wave_size, N_EXPERT * CAP, D)

    def expert_backward(expert):
        rows = in_buf[expert]
        grads = grad_buf[expert]
        summed = jnp.zeros((N_EXPERT * CAP, D), jnp.float32)
        for block in range(SPLIT):
            start = ((expert * SPLIT + block) * FF_DEV).astype(jnp.int32)
            w_first = lax.dynamic_slice_in_dim(w_in, start, FF_DEV, 1)
            w_second = lax.dynamic_slice_in_dim(w_out, start, FF_DEV, 0)
            act = jnp.maximum(jnp.dot(rows, w_first, preferred_element_type=jnp.float32), 0.0).astype(jnp.bfloat16)
            d_act = lax.dot_general(grads, w_second, (((1,), (1,)), ((), ())), preferred_element_type=jnp.float32)
            d_pre = jnp.where(act > 0, d_act, 0.0).astype(jnp.bfloat16)
            d_part = lax.dot_general(d_pre, w_first, (((1,), (1,)), ((), ())), preferred_element_type=jnp.float32).astype(jnp.bfloat16)
            summed = summed + d_part.astype(jnp.float32)
        return summed
    grad_out = lax.map(expert_backward, jnp.arange(wave_size, dtype=jnp.int32)).reshape(total, D)
    d_copy = (grad_out[safe_index] * wave_mask).reshape(TOKENS, 2, D)
    d_normed = d_copy[:, 0] + d_copy[:, 1]
    hidden_grad = (upstream32 + norm_back(normed, scale, d_normed)).astype(jnp.bfloat16)
    return (result, hidden_grad, gate_grad)

def reference(hidden, routes, gates, lengths, w_in, w_out, incoming):
    results = []
    for layer in range(2):
        results.append(one_layer(hidden[layer], routes[layer], gates[layer], lengths[layer], w_in[layer], w_out[layer], incoming[layer], layer))
    outputs = jnp.stack([results[0][0], results[1][0]])
    hidden_grad = jnp.stack([results[0][1], results[1][1]])
    gate_grad = jnp.stack([results[0][2], results[1][2]])
    return (outputs, hidden_grad, gate_grad)
```

```python
import functools

import jax
import jax.numpy as jnp
from jax import lax
from jax.experimental import pallas as pl
from jax.experimental.pallas import tpu as pltpu
from jax.sharding import PartitionSpec as P

SPLIT = 8
CAP = 4
LIVE = 16
SLOTS = LIVE * CAP
EPS = 1e-05
BF = jnp.bfloat16
F32 = jnp.float32
VMEM_LIMIT = 16 * 2**20


def hop(value, step):
    n = lax.axis_size("expert")
    pairs = [(i, i // SPLIT * SPLIT + (i + step) % SPLIT) for i in range(n)]
    return lax.ppermute(value, "expert", pairs)


def swap_plane(rows):
    n = lax.axis_size("expert")
    groups = [[c * SPLIT + p for c in range(n // SPLIT)] for p in range(SPLIT)]
    count, width = rows.shape
    lanes = 128
    packed = rows.reshape(n // SPLIT, count * SPLIT // n * width // lanes, lanes)
    moved = lax.all_to_all(
        packed, "expert", split_axis=0, concat_axis=0, axis_index_groups=groups, tiled=True
    )
    return moved.reshape(count, width)


def gather_ring(block, expert):
    done = expert({0: block})
    up, down = block, block
    for d in range(1, SPLIT // 2):
        up, down = hop(up, 1), hop(down, -1)
        done |= expert({-d: up, d: down})
    return done | expert({"far": hop(up, 1)})


def plus(a, b):
    return (a.astype(F32) + b.astype(F32)).astype(BF)


def scatter_ring(parts):
    up, down = hop(parts["far"], 1), parts[-3]
    for d in range(SPLIT // 2 - 1, 0, -1):
        up = hop(plus(up, parts[d]), 1)
        down = hop(down if d == SPLIT // 2 - 1 else plus(down, parts[-d]), -1)
    return (parts[0].astype(F32) + up.astype(F32) + down.astype(F32)).astype(BF)


def normalize(values):
    center = values - jnp.mean(values, axis=-1, keepdims=True)
    scale = lax.rsqrt(jnp.mean(center * center, axis=-1, keepdims=True) + EPS)
    return center * scale, scale


def norm_back(normed, scale, upstream):
    first = jnp.mean(upstream, axis=-1, keepdims=True)
    second = jnp.mean(upstream * normed, axis=-1, keepdims=True)
    return scale * (upstream - first - normed * second)


def rows_dot(a, b):
    return lax.dot_general(a, b, (((0,), (0,)), ((), ())), preferred_element_type=F32)


def dispatch_kernel(length_ref, routes_ref, hidden_ref, rows_ref, first_ref, second_ref):
    count = hidden_ref.shape[0]
    slot = lax.broadcasted_iota(jnp.int32, (count, SLOTS), 1)
    token = lax.broadcasted_iota(jnp.int32, (count, SLOTS), 0)
    expert, place = slot // CAP, slot % CAP
    alive = token < length_ref[0, 0]
    hit0 = alive & (routes_ref[:, 0:1] == expert)
    hit1 = alive & (routes_ref[:, 1:2] == expert)
    hits = jnp.where(hit0 | hit1, 1.0, 0.0).astype(BF)
    earlier = lax.broadcasted_iota(jnp.int32, (count, count), 1) < lax.broadcasted_iota(
        jnp.int32, (count, count), 0
    )
    rank = jnp.dot(jnp.where(earlier, 1.0, 0.0).astype(BF), hits, preferred_element_type=F32)
    here = rank == place.astype(F32)
    first = jnp.where(hit0 & here, 1.0, 0.0).astype(BF)
    second = jnp.where(hit1 & here, 1.0, 0.0).astype(BF)
    first_ref[...] = first
    second_ref[...] = second
    normed, _ = normalize(hidden_ref[...].astype(F32))
    rows_ref[...] = rows_dot(first + second, normed.astype(BF)).astype(BF)


def middle_kernel(
    info_ref,
    hidden_ref,
    gates_ref,
    first_ref,
    second_ref,
    y_ref,
    keep_ref,
    other_ref,
    result_ref,
    upstream_ref,
    gate_grad_ref,
    rows_ref,
):
    count = hidden_ref.shape[0]
    encoder = info_ref[0] == 0
    alive = lax.broadcasted_iota(jnp.int32, (count, 1), 0) < info_ref[1]
    g0, g1 = gates_ref[:, 0:1], gates_ref[:, 1:2]
    y = y_ref[...]
    y0 = jnp.dot(first_ref[...], y, preferred_element_type=F32)
    y1 = jnp.dot(second_ref[...], y, preferred_element_type=F32)
    layer_out = (hidden_ref[...].astype(F32) + g0 * y0 + g1 * y1).astype(BF)
    hat, scale = normalize(layer_out.astype(F32))
    result_ref[...] = jnp.where(encoder, hat.astype(BF), layer_out)
    keep, other = keep_ref[...].astype(F32), other_ref[...].astype(F32)
    cot = jnp.concatenate(
        [jnp.where(encoder, keep, other), jnp.where(encoder, other, keep)], axis=1
    )
    cot = jnp.where(alive, cot, 0.0)
    upstream = jnp.where(encoder, norm_back(hat, scale, cot), cot).astype(BF)
    upstream_ref[...] = upstream
    up32 = upstream.astype(F32)
    gate_grad_ref[:, 0:1] = jnp.sum(up32 * y0, axis=-1, keepdims=True)
    gate_grad_ref[:, 1:2] = jnp.sum(up32 * y1, axis=-1, keepdims=True)
    rows = rows_dot(first_ref[...], (g0 * up32).astype(BF))
    rows += rows_dot(second_ref[...], (g1 * up32).astype(BF))
    rows_ref[...] = rows.astype(BF)


def final_kernel(hidden_ref, upstream_ref, first_ref, second_ref, d_ref, out_ref):
    normed, scale = normalize(hidden_ref[...].astype(F32))
    both = first_ref[...] + second_ref[...]
    d_normed = jnp.dot(both, d_ref[...], preferred_element_type=F32)
    out_ref[...] = (upstream_ref[...].astype(F32) + norm_back(normed, scale, d_normed)).astype(BF)


def stack(refs):
    return jnp.concatenate([ref[...] for ref in refs], axis=0) if len(refs) > 1 else refs[0][...]


def spread(refs, value):
    start = 0
    for ref in refs:
        ref[...] = value[start : start + ref.shape[0]]
        start += ref.shape[0]


def forward_kernel(count, *refs):
    blocks, (w_in_ref, w_out_ref) = refs[:count], refs[count : count + 2]
    acts, parts = refs[count + 2 : 2 * count + 2], refs[2 * count + 2 :]
    act = jnp.dot(stack(blocks), w_in_ref[...], preferred_element_type=F32)
    act = jnp.maximum(act, 0.0).astype(BF)
    spread(acts, act)
    spread(parts, jnp.dot(act, w_out_ref[...], preferred_element_type=F32).astype(BF))


def backward_kernel(count, *refs):
    blocks, acts, (w_in_t_ref, w_out_t_ref) = (
        refs[:count],
        refs[count : 2 * count],
        refs[2 * count : 2 * count + 2],
    )
    d_act = jnp.dot(stack(blocks), w_out_t_ref[...], preferred_element_type=F32)
    d_pre = jnp.where(stack(acts) > 0, d_act, 0.0).astype(BF)
    part = jnp.dot(d_pre, w_in_t_ref[...], preferred_element_type=F32).astype(BF)
    spread(refs[2 * count + 2 :], part)


def turn_kernel(w_in_ref, w_out_ref, w_in_t_ref, w_out_t_ref):
    w_in_t_ref[...] = w_in_ref[...].T
    w_out_t_ref[...] = w_out_ref[...].T


def call(kernel, outs, scalars, *arrays, flops=0, limit=VMEM_LIMIT):
    vmem = pl.BlockSpec(memory_space=pltpu.VMEM)
    return pl.pallas_call(
        kernel,
        out_shape=outs,
        in_specs=[pl.BlockSpec(memory_space=pltpu.SMEM)] * scalars + [vmem] * (len(arrays) - scalars),
        out_specs=jax.tree.map(lambda _: vmem, outs),
        compiler_params=pltpu.CompilerParams(vmem_limit_bytes=limit),
        cost_estimate=pl.CostEstimate(flops=flops, bytes_accessed=2**20, transcendentals=0),
    )(*arrays)


def per_device(hidden, routes, gates, lengths, w_in, w_out, incoming):
    section = lax.axis_index("section")
    source, w_in, w_out = hidden[0], w_in[0], w_out[0]
    count, width = source.shape
    wide = jax.ShapeDtypeStruct((count, width), BF)
    slots = jax.ShapeDtypeStruct((SLOTS, width), BF)
    table = jax.ShapeDtypeStruct((count, SLOTS), BF)

    keep = jnp.where(section == 0, incoming[0], incoming[1])
    send = jnp.where(section == 0, incoming[1], incoming[0])
    other = lax.ppermute(send, "section", [(0, 1), (1, 0)])

    rows, first, second = call(
        dispatch_kernel, [slots, table, table], 1, lengths, routes[0], source
    )

    turned = [jax.ShapeDtypeStruct(w.shape[::-1], BF) for w in (w_in, w_out)]
    w_in_t, w_out_t = call(turn_kernel, turned, 0, w_in, w_out, limit=32 * 2**20)
    hidden_units = w_in.shape[1]
    acts = {}

    def forward(blocks):
        n = len(blocks)
        outs = [jax.ShapeDtypeStruct((b.shape[0], hidden_units), BF) for b in blocks.values()]
        outs += [jax.ShapeDtypeStruct(b.shape, BF) for b in blocks.values()]
        got = call(
            functools.partial(forward_kernel, n),
            outs,
            0,
            *blocks.values(),
            w_in,
            w_out,
            flops=4 * n * SLOTS * width * hidden_units,
            limit=32 * 2**20,
        )
        acts.update(zip(blocks, got[:n]))
        return dict(zip(blocks, got[n:]))

    def backward(blocks):
        n = len(blocks)
        got = call(
            functools.partial(backward_kernel, n),
            [jax.ShapeDtypeStruct(b.shape, BF) for b in blocks.values()],
            0,
            *blocks.values(),
            *[acts[d] for d in blocks],
            w_in_t,
            w_out_t,
            flops=4 * n * SLOTS * width * hidden_units,
            limit=32 * 2**20,
        )
        return dict(zip(blocks, got))

    y = swap_plane(scatter_ring(gather_ring(swap_plane(rows), forward)))

    info = jnp.stack([section.astype(jnp.int32), lengths[0, 0]])
    result, upstream, gate_grad, grad_rows = call(
        middle_kernel,
        [wide, wide, jax.ShapeDtypeStruct((count, 2), F32), slots],
        1,
        info,
        source,
        gates[0],
        first,
        second,
        y,
        keep,
        other,
    )

    d_rows = swap_plane(scatter_ring(gather_ring(swap_plane(grad_rows), backward)))

    hidden_grad = call(final_kernel, wide, 0, source, upstream, first, second, d_rows)
    return (result[None], hidden_grad[None], gate_grad[None])


def solution(mesh):
    in_specs = (
        P("section", "expert", None),
        P("section", "expert", None),
        P("section", "expert", None),
        P("section", "expert"),
        P("section", None, "expert"),
        P("section", "expert", None),
        P(None, "expert", "section"),
    )
    out_specs = (
        P("section", "expert", None),
        P("section", "expert", None),
        P("section", "expert", None),
    )
    return jax.shard_map(
        per_device, mesh=mesh, in_specs=in_specs, out_specs=out_specs, check_vma=False
    )
```

```python
import functools

import jax
import jax.numpy as jnp
from jax import lax
from jax.experimental import pallas as pl
from jax.experimental.pallas import tpu as pltpu
from jax.sharding import PartitionSpec as P

SPLIT = 8
CAP = 4
LIVE = 16
SLOTS = LIVE * CAP
EPS = 1e-05
COST = 32
BF = jnp.bfloat16
F32 = jnp.float32
VMEM_LIMIT = 16 * 2**20


def hop(value, step):
    n = lax.axis_size("expert")
    pairs = [(i, i // SPLIT * SPLIT + (i + step) % SPLIT) for i in range(n)]
    return lax.ppermute(value, "expert", pairs)


def swap_plane(rows):
    n = lax.axis_size("expert")
    groups = [[c * SPLIT + p for c in range(n // SPLIT)] for p in range(SPLIT)]
    count, width = rows.shape
    lanes = 128
    packed = rows.reshape(n // SPLIT, count * SPLIT // n * width // lanes, lanes)
    moved = lax.all_to_all(
        packed, "expert", split_axis=0, concat_axis=0, axis_index_groups=groups, tiled=True
    )
    return moved.reshape(count, width)


def swap_pair(rows):
    n = lax.axis_size("expert")
    half = SPLIT // 2
    groups = [[c * SPLIT + q for q in (p, p + half) for c in range(n // SPLIT)] for p in range(half)]
    count, width = rows.shape
    lanes = 128
    packed = rows.reshape(len(groups[0]), count * width // lanes // len(groups[0]), lanes)
    moved = lax.all_to_all(
        packed, "expert", split_axis=0, concat_axis=0, axis_index_groups=groups, tiled=True
    )
    return moved.reshape(count, width)


def nearer(pair, flip):
    half = pair.shape[0] // 2
    return jnp.where(flip, pair[half:], pair[:half])


def exchange(rows, flips, expert):
    pair = swap_pair(rows)
    up, down = hop(pair, 1), hop(pair, -1)
    ((own, across),) = expert(0, [pair])
    sum_up = hop(across, 1)
    up_2, down_2 = hop(nearer(up, flips[1] == 1), 1), hop(nearer(down, flips[2] == 1), -1)
    (low_1, high_3), (high_1, low_3) = expert(1, [up, down])
    sum_up, sum_down = hop(plus(sum_up, high_3), 1), hop(low_3, -1)
    low_2, high_2 = expert(2, [up_2, down_2])
    sum_up, sum_down = hop(plus(sum_up, high_2), 1), hop(plus(sum_down, low_2), -1)
    sum_up, sum_down = hop(plus(sum_up, high_1), 1), hop(plus(sum_down, low_1), -1)
    return (own.astype(F32) + sum_up.astype(F32) + sum_down.astype(F32)).astype(BF)


def plus(a, b):
    return (a.astype(F32) + b.astype(F32)).astype(BF)


def normalize(values):
    center = values - jnp.mean(values, axis=-1, keepdims=True)
    scale = lax.rsqrt(jnp.mean(center * center, axis=-1, keepdims=True) + EPS)
    return center * scale, scale


def norm_back(normed, scale, upstream):
    first = jnp.mean(upstream, axis=-1, keepdims=True)
    second = jnp.mean(upstream * normed, axis=-1, keepdims=True)
    return scale * (upstream - first - normed * second)


def rows_dot(a, b):
    return lax.dot_general(a, b, (((0,), (0,)), ((), ())), preferred_element_type=F32)


def column(row):
    return jnp.broadcast_to(row, (row.shape[1], row.shape[1])).T[:, 0:1]


def row(column):
    return jnp.broadcast_to(column, (column.shape[0], column.shape[0])).T[0:1, :]


def dispatch_kernel(length_ref, section_ref, routes_ref, hidden_ref, rows_ref, first_ref, second_ref):
    count = hidden_ref.shape[0]
    slot = lax.broadcasted_iota(jnp.int32, (SLOTS, count), 0)
    token = lax.broadcasted_iota(jnp.int32, (SLOTS, count), 1)
    expert, place = slot // CAP, slot % CAP
    alive = token < length_ref[0, 0]
    hit0 = alive & (routes_ref[0:1, :] == expert)
    hit1 = alive & (routes_ref[1:2, :] == expert)
    hits = jnp.where(hit0 | hit1, 1.0, 0.0).astype(BF)
    earlier = lax.broadcasted_iota(jnp.int32, (count, count), 0) < lax.broadcasted_iota(
        jnp.int32, (count, count), 1
    )
    rank = jnp.dot(hits, jnp.where(earlier, 1.0, 0.0).astype(BF), preferred_element_type=F32)
    here = rank == place.astype(F32)
    first = jnp.where(hit0 & here, 1.0, 0.0).astype(BF)
    second = jnp.where(hit1 & here, 1.0, 0.0).astype(BF)
    first_ref[...] = first
    second_ref[...] = second
    normed, _ = normalize(hidden_ref[...].astype(F32))
    rows = jnp.dot(first + second, normed.astype(BF), preferred_element_type=F32).astype(BF)
    rows_ref[:SLOTS] = rows
    rows_ref[SLOTS:] = rows


def middle_kernel(
    length_ref,
    section_ref,
    hidden_ref,
    gates_ref,
    first_ref,
    second_ref,
    y_ref,
    keep_ref,
    other_ref,
    result_ref,
    upstream_ref,
    gate_grad_ref,
    rows_ref,
):
    count = hidden_ref.shape[0]
    encoder = section_ref[0] == 0
    alive = lax.broadcasted_iota(jnp.int32, (count, 1), 0) < length_ref[0, 0]
    g0, g1 = column(gates_ref[0:1, :]), column(gates_ref[1:2, :])
    y = y_ref[...]
    y0 = rows_dot(first_ref[...], y)
    y1 = rows_dot(second_ref[...], y)
    layer_out = (hidden_ref[...].astype(F32) + g0 * y0 + g1 * y1).astype(BF)
    hat, scale = normalize(layer_out.astype(F32))
    result_ref[...] = jnp.where(encoder, hat.astype(BF), layer_out)
    keep, other = keep_ref[...].astype(F32), other_ref[...].astype(F32)
    cot = jnp.concatenate(
        [jnp.where(encoder, keep, other), jnp.where(encoder, other, keep)], axis=1
    )
    cot = jnp.where(alive, cot, 0.0)
    upstream = jnp.where(encoder, norm_back(hat, scale, cot), cot).astype(BF)
    upstream_ref[...] = upstream
    up32 = upstream.astype(F32)
    gate_grad_ref[0:1, :] = row(jnp.sum(up32 * y0, axis=-1, keepdims=True))
    gate_grad_ref[1:2, :] = row(jnp.sum(up32 * y1, axis=-1, keepdims=True))
    rows = jnp.dot(first_ref[...], (g0 * up32).astype(BF), preferred_element_type=F32)
    rows += jnp.dot(second_ref[...], (g1 * up32).astype(BF), preferred_element_type=F32)
    rows_ref[:SLOTS] = rows.astype(BF)
    rows_ref[SLOTS:] = rows.astype(BF)


def final_kernel(hidden_ref, upstream_ref, first_ref, second_ref, d_ref, out_ref):
    normed, scale = normalize(hidden_ref[...].astype(F32))
    d_normed = rows_dot(first_ref[...] + second_ref[...], d_ref[...])
    out_ref[...] = (upstream_ref[...].astype(F32) + norm_back(normed, scale, d_normed)).astype(BF)


def stack(refs):
    return jnp.concatenate([ref[...] for ref in refs], axis=0) if len(refs) > 1 else refs[0][...]


def spread(refs, terms, flip_ref, start):
    rows = refs[0].shape[0]
    for i in range(0, len(refs), 1 if start is None else 2):
        part = terms[i * rows : (i + 1) * rows]
        if start is None:
            refs[i][...] = part.astype(BF)
            continue
        other = terms[(i + 1) * rows : (i + 2) * rows]
        flip = flip_ref[start + i // 2] == 1
        refs[i][...] = jnp.where(flip, other, part).astype(BF)
        refs[i + 1][...] = jnp.where(flip, part, other).astype(BF)


def forward_kernel(count, start, flip_ref, *refs):
    blocks, (w_in_ref, w_out_ref) = refs[:count], refs[count : count + 2]
    act_ref, parts = refs[count + 2], refs[count + 3 :]
    act = jnp.dot(stack(blocks), w_in_ref[...], preferred_element_type=F32)
    act = jnp.maximum(act, 0.0).astype(BF)
    act_ref[...] = act
    spread(parts, jnp.dot(act, w_out_ref[...], preferred_element_type=F32), flip_ref, start)


def backward_kernel(count, start, flip_ref, *refs):
    blocks, (act_ref, w_in_t_ref, w_out_t_ref) = refs[:count], refs[count : count + 3]
    d_act = jnp.dot(stack(blocks), w_out_t_ref[...], preferred_element_type=F32)
    d_pre = jnp.where(act_ref[...] > 0, d_act, 0.0).astype(BF)
    terms = jnp.dot(d_pre, w_in_t_ref[...], preferred_element_type=F32)
    spread(refs[count + 3 :], terms, flip_ref, start)


def turn_kernel(w_in_ref, w_out_ref, w_in_t_ref, w_out_t_ref):
    w_in_t_ref[...] = w_in_ref[...].T
    w_out_t_ref[...] = w_out_ref[...].T


def call(kernel, outs, scalars, *arrays, flops=0, limit=VMEM_LIMIT):
    vmem = pl.BlockSpec(memory_space=pltpu.VMEM)
    return pl.pallas_call(
        kernel,
        out_shape=outs,
        in_specs=[pl.BlockSpec(memory_space=pltpu.SMEM)] * scalars + [vmem] * (len(arrays) - scalars),
        out_specs=jax.tree.map(lambda _: vmem, outs),
        compiler_params=pltpu.CompilerParams(vmem_limit_bytes=limit),
        cost_estimate=pl.CostEstimate(flops=flops, bytes_accessed=2**20, transcendentals=0),
    )(*arrays)


def per_device(hidden, routes, gates, lengths, w_in, w_out, incoming):
    section = lax.axis_index("section")
    source, w_in, w_out = hidden[0], w_in[0], w_out[0]
    count, width = source.shape
    wide = jax.ShapeDtypeStruct((count, width), BF)
    slots = jax.ShapeDtypeStruct((SLOTS, width), BF)
    twice = jax.ShapeDtypeStruct((2 * SLOTS, width), BF)
    table = jax.ShapeDtypeStruct((SLOTS, count), BF)
    section_id = jnp.reshape(section.astype(jnp.int32), (1,))

    keep = jnp.where(section == 0, incoming[0], incoming[1])
    send = jnp.where(section == 0, incoming[1], incoming[0])
    other = lax.ppermute(send, "section", [(0, 1), (1, 0)])

    rows, first, second = call(
        dispatch_kernel, [twice, table, table], 2, lengths, section_id, routes[0].T, source
    )

    turned = [jax.ShapeDtypeStruct(w.shape[::-1], BF) for w in (w_in, w_out)]
    w_in_t, w_out_t = call(turn_kernel, turned, 0, w_in, w_out, limit=32 * 2**20)
    hidden_units = w_in.shape[1]
    plane = lax.axis_index("expert") % SPLIT
    flips = jnp.stack([(plane + d) % SPLIT // (SPLIT // 2) for d in (0, -1, 1)]).astype(jnp.int32)
    acts = {}

    def run(kernel, key, blocks, extra, outs):
        start = (0, 1, None)[key]
        total = sum(b.shape[0] for b in blocks)
        outs = outs + [slots] * (total // SLOTS)
        got = call(
            functools.partial(kernel, len(blocks), start),
            outs,
            1,
            flips,
            *blocks,
            *extra,
            flops=COST * total * width * hidden_units,
        )
        terms = got[len(outs) - total // SLOTS :]
        return got, terms if start is None else list(zip(terms[::2], terms[1::2]))

    def forward(key, blocks):
        total = sum(b.shape[0] for b in blocks)
        outs = [jax.ShapeDtypeStruct((total, hidden_units), BF)]
        got, terms = run(forward_kernel, key, blocks, [w_in, w_out], outs)
        acts[key] = got[0]
        return terms

    def backward(key, blocks):
        return run(backward_kernel, key, blocks, [acts[key], w_in_t, w_out_t], [])[1]

    y = swap_plane(exchange(rows, flips, forward))

    result, upstream, gate_grad, grad_rows = call(
        middle_kernel,
        [wide, wide, jax.ShapeDtypeStruct((2, count), F32), twice],
        2,
        lengths,
        section_id,
        source,
        gates[0].T,
        first,
        second,
        y,
        keep,
        other,
    )

    d_rows = swap_plane(exchange(grad_rows, flips, backward))

    hidden_grad = call(final_kernel, wide, 0, source, upstream, first, second, d_rows)
    return (result[None], hidden_grad[None], gate_grad.T[None])


def solution(mesh):
    in_specs = (
        P("section", "expert", None),
        P("section", "expert", None),
        P("section", "expert", None),
        P("section", "expert"),
        P("section", None, "expert"),
        P("section", "expert", None),
        P(None, "expert", "section"),
    )
    out_specs = (
        P("section", "expert", None),
        P("section", "expert", None),
        P("section", "expert", None),
    )
    return jax.shard_map(
        per_device, mesh=mesh, in_specs=in_specs, out_specs=out_specs, check_vma=False
    )
```

```python
import functools

import jax
import jax.numpy as jnp
from jax import lax
from jax.experimental import pallas as pl
from jax.experimental.pallas import tpu as pltpu
from jax.sharding import PartitionSpec as P

SPLIT = 8
CAP = 4
LIVE = 16
SLOTS = LIVE * CAP
EPS = 1e-05
COST = 4
BF = jnp.bfloat16
F32 = jnp.float32
VMEM_LIMIT = 16 * 2**20


def hop(value, step):
    n = lax.axis_size("expert")
    pairs = [(i, i // SPLIT * SPLIT + (i + step) % SPLIT) for i in range(n)]
    return lax.ppermute(value, "expert", pairs)


def swap_plane(rows):
    n = lax.axis_size("expert")
    groups = [[c * SPLIT + p for c in range(n // SPLIT)] for p in range(SPLIT)]
    count, width = rows.shape
    lanes = 128
    packed = rows.reshape(n // SPLIT, count * SPLIT // n * width // lanes, lanes)
    moved = lax.all_to_all(
        packed, "expert", split_axis=0, concat_axis=0, axis_index_groups=groups, tiled=True
    )
    return moved.reshape(count, width)


def swap_pair(rows):
    n = lax.axis_size("expert")
    half = SPLIT // 2
    groups = [[c * SPLIT + q for q in (p, p + half) for c in range(n // SPLIT)] for p in range(half)]
    count, width = rows.shape
    lanes = 128
    packed = rows.reshape(len(groups[0]), count * width // lanes // len(groups[0]), lanes)
    moved = lax.all_to_all(
        packed, "expert", split_axis=0, concat_axis=0, axis_index_groups=groups, tiled=True
    )
    return moved.reshape(count, width)


def nearer(pair, flip):
    half = pair.shape[0] // 2
    return jnp.where(flip, pair[half:], pair[:half])


def exchange(rows, flips, expert):
    pair = swap_pair(rows)
    up, down = hop(pair, 1), hop(pair, -1)
    ((own, across),) = expert(0, [pair])
    sum_up = hop(across, 1)
    up_2, down_2 = hop(nearer(up, flips[1] == 1), 1), hop(nearer(down, flips[2] == 1), -1)
    (low_1, high_3), (high_1, low_3) = expert(1, [up, down])
    sum_up, sum_down = hop(plus(sum_up, high_3), 1), hop(low_3, -1)
    low_2, high_2 = expert(2, [up_2, down_2])
    sum_up, sum_down = hop(plus(sum_up, high_2), 1), hop(plus(sum_down, low_2), -1)
    sum_up, sum_down = hop(plus(sum_up, high_1), 1), hop(plus(sum_down, low_1), -1)
    return (own.astype(F32) + sum_up.astype(F32) + sum_down.astype(F32)).astype(BF)


def plus(a, b):
    return (a.astype(F32) + b.astype(F32)).astype(BF)


def normalize(values):
    center = values - jnp.mean(values, axis=-1, keepdims=True)
    scale = lax.rsqrt(jnp.mean(center * center, axis=-1, keepdims=True) + EPS)
    return center * scale, scale


def norm_back(normed, scale, upstream):
    first = jnp.mean(upstream, axis=-1, keepdims=True)
    second = jnp.mean(upstream * normed, axis=-1, keepdims=True)
    return scale * (upstream - first - normed * second)


def rows_dot(a, b):
    return lax.dot_general(a, b, (((0,), (0,)), ((), ())), preferred_element_type=F32)


def column(row):
    return jnp.broadcast_to(row, (row.shape[1], row.shape[1])).T[:, 0:1]


def row(column):
    return jnp.broadcast_to(column, (column.shape[0], column.shape[0])).T[0:1, :]


def dispatch_kernel(length_ref, section_ref, routes_ref, hidden_ref, rows_ref, first_ref, second_ref):
    count = hidden_ref.shape[0]
    slot = lax.broadcasted_iota(jnp.int32, (SLOTS, count), 0)
    token = lax.broadcasted_iota(jnp.int32, (SLOTS, count), 1)
    expert, place = slot // CAP, slot % CAP
    alive = token < length_ref[0, 0]
    hit0 = alive & (routes_ref[0:1, :] == expert)
    hit1 = alive & (routes_ref[1:2, :] == expert)
    hits = jnp.where(hit0 | hit1, 1.0, 0.0).astype(BF)
    earlier = lax.broadcasted_iota(jnp.int32, (count, count), 0) < lax.broadcasted_iota(
        jnp.int32, (count, count), 1
    )
    rank = jnp.dot(hits, jnp.where(earlier, 1.0, 0.0).astype(BF), preferred_element_type=F32)
    here = rank == place.astype(F32)
    first = jnp.where(hit0 & here, 1.0, 0.0).astype(BF)
    second = jnp.where(hit1 & here, 1.0, 0.0).astype(BF)
    first_ref[...] = first
    second_ref[...] = second
    normed, _ = normalize(hidden_ref[...].astype(F32))
    rows = jnp.dot(first + second, normed.astype(BF), preferred_element_type=F32).astype(BF)
    rows_ref[:SLOTS] = rows
    rows_ref[SLOTS:] = rows


def middle_kernel(
    length_ref,
    section_ref,
    hidden_ref,
    gates_ref,
    first_ref,
    second_ref,
    y_ref,
    keep_ref,
    other_ref,
    result_ref,
    upstream_ref,
    gate_grad_ref,
    rows_ref,
):
    count = hidden_ref.shape[0]
    encoder = section_ref[0] == 0
    alive = lax.broadcasted_iota(jnp.int32, (count, 1), 0) < length_ref[0, 0]
    g0, g1 = column(gates_ref[0:1, :]), column(gates_ref[1:2, :])
    y = y_ref[...]
    y0 = rows_dot(first_ref[...], y)
    y1 = rows_dot(second_ref[...], y)
    layer_out = (hidden_ref[...].astype(F32) + g0 * y0 + g1 * y1).astype(BF)
    hat, scale = normalize(layer_out.astype(F32))
    result_ref[...] = jnp.where(encoder, hat.astype(BF), layer_out)
    keep, other = keep_ref[...].astype(F32), other_ref[...].astype(F32)
    cot = jnp.concatenate(
        [jnp.where(encoder, keep, other), jnp.where(encoder, other, keep)], axis=1
    )
    cot = jnp.where(alive, cot, 0.0)
    upstream = jnp.where(encoder, norm_back(hat, scale, cot), cot).astype(BF)
    upstream_ref[...] = upstream
    up32 = upstream.astype(F32)
    gate_grad_ref[0:1, :] = row(jnp.sum(up32 * y0, axis=-1, keepdims=True))
    gate_grad_ref[1:2, :] = row(jnp.sum(up32 * y1, axis=-1, keepdims=True))
    rows = jnp.dot(first_ref[...], (g0 * up32).astype(BF), preferred_element_type=F32)
    rows += jnp.dot(second_ref[...], (g1 * up32).astype(BF), preferred_element_type=F32)
    rows_ref[:SLOTS] = rows.astype(BF)
    rows_ref[SLOTS:] = rows.astype(BF)


def final_kernel(hidden_ref, upstream_ref, first_ref, second_ref, d_ref, out_ref):
    normed, scale = normalize(hidden_ref[...].astype(F32))
    d_normed = rows_dot(first_ref[...] + second_ref[...], d_ref[...])
    out_ref[...] = (upstream_ref[...].astype(F32) + norm_back(normed, scale, d_normed)).astype(BF)


def turned_dot(a, b):
    return lax.dot_general(a, b, (((1,), (1,)), ((), ())), preferred_element_type=F32)


def stack(refs):
    return jnp.concatenate([ref[...] for ref in refs], axis=0) if len(refs) > 1 else refs[0][...]


def spread(refs, terms, flip_ref, start):
    rows = refs[0].shape[0]
    for i in range(0, len(refs), 1 if start is None else 2):
        part = terms[i * rows : (i + 1) * rows]
        if start is None:
            refs[i][...] = part.astype(BF)
            continue
        other = terms[(i + 1) * rows : (i + 2) * rows]
        flip = flip_ref[start + i // 2] == 1
        refs[i][...] = jnp.where(flip, other, part).astype(BF)
        refs[i + 1][...] = jnp.where(flip, part, other).astype(BF)


def forward_kernel(count, start, flip_ref, *refs):
    blocks, (w_in_ref, w_out_ref) = refs[:count], refs[count : count + 2]
    act_ref, parts = refs[count + 2], refs[count + 3 :]
    act = jnp.dot(stack(blocks), w_in_ref[...], preferred_element_type=F32)
    act = jnp.maximum(act, 0.0).astype(BF)
    act_ref[...] = act
    spread(parts, jnp.dot(act, w_out_ref[...], preferred_element_type=F32), flip_ref, start)


def backward_kernel(count, start, flip_ref, *refs):
    blocks, (act_ref, w_in_ref, w_out_ref) = refs[:count], refs[count : count + 3]
    d_act = turned_dot(stack(blocks), w_out_ref[...])
    d_pre = jnp.where(act_ref[...] > 0, d_act, 0.0).astype(BF)
    terms = turned_dot(d_pre, w_in_ref[...])
    spread(refs[count + 3 :], terms, flip_ref, start)


def call(kernel, outs, scalars, *arrays, flops=0, limit=VMEM_LIMIT):
    vmem = pl.BlockSpec(memory_space=pltpu.VMEM)
    return pl.pallas_call(
        kernel,
        out_shape=outs,
        in_specs=[pl.BlockSpec(memory_space=pltpu.SMEM)] * scalars + [vmem] * (len(arrays) - scalars),
        out_specs=jax.tree.map(lambda _: vmem, outs),
        compiler_params=pltpu.CompilerParams(vmem_limit_bytes=limit),
        cost_estimate=pl.CostEstimate(flops=flops, bytes_accessed=2**20, transcendentals=0),
    )(*arrays)


def per_device(hidden, routes, gates, lengths, w_in, w_out, incoming):
    section = lax.axis_index("section")
    source, w_in, w_out = hidden[0], w_in[0], w_out[0]
    count, width = source.shape
    wide = jax.ShapeDtypeStruct((count, width), BF)
    slots = jax.ShapeDtypeStruct((SLOTS, width), BF)
    twice = jax.ShapeDtypeStruct((2 * SLOTS, width), BF)
    table = jax.ShapeDtypeStruct((SLOTS, count), BF)
    section_id = jnp.reshape(section.astype(jnp.int32), (1,))

    keep = jnp.where(section == 0, incoming[0], incoming[1])
    send = jnp.where(section == 0, incoming[1], incoming[0])
    other = lax.ppermute(send, "section", [(0, 1), (1, 0)])

    rows, first, second = call(
        dispatch_kernel, [twice, table, table], 2, lengths, section_id, routes[0].T, source
    )

    hidden_units = w_in.shape[1]
    plane = lax.axis_index("expert") % SPLIT
    flips = jnp.stack([(plane + d) % SPLIT // (SPLIT // 2) for d in (0, -1, 1)]).astype(jnp.int32)
    acts = {}

    def run(kernel, key, blocks, extra, outs):
        start = (0, 1, None)[key]
        total = sum(b.shape[0] for b in blocks)
        outs = outs + [slots] * (total // SLOTS)
        got = call(
            functools.partial(kernel, len(blocks), start),
            outs,
            1,
            flips,
            *blocks,
            *extra,
            flops=COST * total * width * hidden_units,
        )
        terms = got[len(outs) - total // SLOTS :]
        return got, terms if start is None else list(zip(terms[::2], terms[1::2]))

    def forward(key, blocks):
        total = sum(b.shape[0] for b in blocks)
        outs = [jax.ShapeDtypeStruct((total, hidden_units), BF)]
        got, terms = run(forward_kernel, key, blocks, [w_in, w_out], outs)
        acts[key] = got[0]
        return terms

    def backward(key, blocks):
        return run(backward_kernel, key, blocks, [acts[key], w_in, w_out], [])[1]

    y = swap_plane(exchange(rows, flips, forward))

    result, upstream, gate_grad, grad_rows = call(
        middle_kernel,
        [wide, wide, jax.ShapeDtypeStruct((2, count), F32), twice],
        2,
        lengths,
        section_id,
        source,
        gates[0].T,
        first,
        second,
        y,
        keep,
        other,
    )

    d_rows = swap_plane(exchange(grad_rows, flips, backward))

    hidden_grad = call(final_kernel, wide, 0, source, upstream, first, second, d_rows)
    return (result[None], hidden_grad[None], gate_grad.T[None])


def solution(mesh):
    in_specs = (
        P("section", "expert", None),
        P("section", "expert", None),
        P("section", "expert", None),
        P("section", "expert"),
        P("section", None, "expert"),
        P("section", "expert", None),
        P(None, "expert", "section"),
    )
    out_specs = (
        P("section", "expert", None),
        P("section", "expert", None),
        P("section", "expert", None),
    )
    return jax.shard_map(
        per_device, mesh=mesh, in_specs=in_specs, out_specs=out_specs, check_vma=False
    )
```

```python
import functools

import jax
import jax.numpy as jnp
from jax import lax
from jax.experimental import pallas as pl
from jax.experimental.pallas import tpu as pltpu
from jax.sharding import PartitionSpec as P

SPLIT = 8
CAP = 4
LIVE = 16
SLOTS = LIVE * CAP
EPS = 1e-05
COST = 1
BF = jnp.bfloat16
F32 = jnp.float32
VMEM_LIMIT = 16 * 2**20


def hop(value, step):
    n = lax.axis_size("expert")
    pairs = [(i, i // SPLIT * SPLIT + (i + step) % SPLIT) for i in range(n)]
    return lax.ppermute(value, "expert", pairs)


def swap_plane(rows):
    n = lax.axis_size("expert")
    groups = [[c * SPLIT + p for c in range(n // SPLIT)] for p in range(SPLIT)]
    count, width = rows.shape
    lanes = 128
    packed = rows.reshape(n // SPLIT, count * SPLIT // n * width // lanes, lanes)
    moved = lax.all_to_all(
        packed, "expert", split_axis=0, concat_axis=0, axis_index_groups=groups, tiled=True
    )
    return moved.reshape(count, width)


def swap_pair(rows):
    n = lax.axis_size("expert")
    half = SPLIT // 2
    groups = [[c * SPLIT + q for q in (p, p + half) for c in range(n // SPLIT)] for p in range(half)]
    count, width = rows.shape
    lanes = 128
    packed = rows.reshape(len(groups[0]), count * width // lanes // len(groups[0]), lanes)
    moved = lax.all_to_all(
        packed, "expert", split_axis=0, concat_axis=0, axis_index_groups=groups, tiled=True
    )
    return moved.reshape(count, width)


def nearer(pair, flip):
    half = pair.shape[0] // 2
    return jnp.where(flip, pair[half:], pair[:half])


def exchange(rows, flips, expert, ahead=()):
    pair = swap_pair(rows)
    up, down = hop(pair, 1), hop(pair, -1)
    if ahead:
        up, *ahead = lax.optimization_barrier((up, *ahead))
    ((own, across),) = expert(0, [pair])
    sum_up = hop(across, 1)
    up_2, down_2 = hop(nearer(up, flips[1] == 1), 1), hop(nearer(down, flips[2] == 1), -1)
    (low_1, high_3), (high_1, low_3) = expert(1, [up, down])
    sum_up, sum_down = hop(plus(sum_up, high_3), 1), hop(low_3, -1)
    low_2, high_2 = expert(2, [up_2, down_2])
    sum_up, sum_down = hop(plus(sum_up, high_2), 1), hop(plus(sum_down, low_2), -1)
    sum_up, sum_down = hop(plus(sum_up, high_1), 1), hop(plus(sum_down, low_1), -1)
    total = own.astype(F32) + sum_up.astype(F32) + sum_down.astype(F32)
    return total.astype(BF), ahead


def plus(a, b):
    return (a.astype(F32) + b.astype(F32)).astype(BF)


def normalize(values):
    center = values - jnp.mean(values, axis=-1, keepdims=True)
    scale = lax.rsqrt(jnp.mean(center * center, axis=-1, keepdims=True) + EPS)
    return center * scale, scale


def norm_back(normed, scale, upstream):
    first = jnp.mean(upstream, axis=-1, keepdims=True)
    second = jnp.mean(upstream * normed, axis=-1, keepdims=True)
    return scale * (upstream - first - normed * second)


def rows_dot(a, b):
    return lax.dot_general(a, b, (((0,), (0,)), ((), ())), preferred_element_type=F32)


def column(row):
    return jnp.broadcast_to(row, (row.shape[1], row.shape[1])).T[:, 0:1]


def row(column):
    return jnp.broadcast_to(column, (column.shape[0], column.shape[0])).T[0:1, :]


def dispatch_kernel(length_ref, section_ref, routes_ref, hidden_ref, rows_ref, first_ref, second_ref):
    count = hidden_ref.shape[0]
    slot = lax.broadcasted_iota(jnp.int32, (SLOTS, count), 0)
    token = lax.broadcasted_iota(jnp.int32, (SLOTS, count), 1)
    expert, place = slot // CAP, slot % CAP
    alive = token < length_ref[0, 0]
    hit0 = alive & (routes_ref[0:1, :] == expert)
    hit1 = alive & (routes_ref[1:2, :] == expert)
    hits = jnp.where(hit0 | hit1, 1.0, 0.0).astype(BF)
    earlier = lax.broadcasted_iota(jnp.int32, (count, count), 0) < lax.broadcasted_iota(
        jnp.int32, (count, count), 1
    )
    rank = jnp.dot(hits, jnp.where(earlier, 1.0, 0.0).astype(BF), preferred_element_type=F32)
    here = rank == place.astype(F32)
    first = jnp.where(hit0 & here, 1.0, 0.0).astype(BF)
    second = jnp.where(hit1 & here, 1.0, 0.0).astype(BF)
    first_ref[...] = first
    second_ref[...] = second
    normed, _ = normalize(hidden_ref[...].astype(F32))
    rows = jnp.dot(first + second, normed.astype(BF), preferred_element_type=F32).astype(BF)
    rows_ref[:SLOTS] = rows
    rows_ref[SLOTS:] = rows


def middle_kernel(
    length_ref,
    section_ref,
    hidden_ref,
    gates_ref,
    first_ref,
    second_ref,
    y_ref,
    keep_ref,
    other_ref,
    result_ref,
    upstream_ref,
    gate_grad_ref,
    rows_ref,
):
    count = hidden_ref.shape[0]
    encoder = section_ref[0] == 0
    alive = lax.broadcasted_iota(jnp.int32, (count, 1), 0) < length_ref[0, 0]
    g0, g1 = column(gates_ref[0:1, :]), column(gates_ref[1:2, :])
    y = y_ref[...]
    y0 = rows_dot(first_ref[...], y)
    y1 = rows_dot(second_ref[...], y)
    layer_out = (hidden_ref[...].astype(F32) + g0 * y0 + g1 * y1).astype(BF)
    hat, scale = normalize(layer_out.astype(F32))
    result_ref[...] = jnp.where(encoder, hat.astype(BF), layer_out)
    keep, other = keep_ref[...].astype(F32), other_ref[...].astype(F32)
    cot = jnp.concatenate(
        [jnp.where(encoder, keep, other), jnp.where(encoder, other, keep)], axis=1
    )
    cot = jnp.where(alive, cot, 0.0)
    upstream = jnp.where(encoder, norm_back(hat, scale, cot), cot).astype(BF)
    upstream_ref[...] = upstream
    up32 = upstream.astype(F32)
    gate_grad_ref[0:1, :] = row(jnp.sum(up32 * y0, axis=-1, keepdims=True))
    gate_grad_ref[1:2, :] = row(jnp.sum(up32 * y1, axis=-1, keepdims=True))
    rows = jnp.dot(first_ref[...], (g0 * up32).astype(BF), preferred_element_type=F32)
    rows += jnp.dot(second_ref[...], (g1 * up32).astype(BF), preferred_element_type=F32)
    rows_ref[:SLOTS] = rows.astype(BF)
    rows_ref[SLOTS:] = rows.astype(BF)


def final_kernel(hidden_ref, upstream_ref, first_ref, second_ref, d_ref, out_ref):
    normed, scale = normalize(hidden_ref[...].astype(F32))
    d_normed = rows_dot(first_ref[...] + second_ref[...], d_ref[...])
    out_ref[...] = (upstream_ref[...].astype(F32) + norm_back(normed, scale, d_normed)).astype(BF)


def turned_dot(a, b):
    return lax.dot_general(a, b, (((1,), (1,)), ((), ())), preferred_element_type=F32)


def stack(refs):
    return jnp.concatenate([ref[...] for ref in refs], axis=0) if len(refs) > 1 else refs[0][...]


def spread(refs, terms, flip_ref, start):
    rows = refs[0].shape[0]
    for i in range(0, len(refs), 1 if start is None else 2):
        part = terms[i * rows : (i + 1) * rows]
        if start is None:
            refs[i][...] = part.astype(BF)
            continue
        other = terms[(i + 1) * rows : (i + 2) * rows]
        flip = flip_ref[start + i // 2] == 1
        refs[i][...] = jnp.where(flip, other, part).astype(BF)
        refs[i + 1][...] = jnp.where(flip, part, other).astype(BF)


def forward_kernel(count, start, flip_ref, *refs):
    blocks, (w_in_ref, w_out_ref) = refs[:count], refs[count : count + 2]
    act_ref, parts = refs[count + 2], refs[count + 3 :]
    act = jnp.dot(stack(blocks), w_in_ref[...], preferred_element_type=F32)
    act = jnp.maximum(act, 0.0).astype(BF)
    act_ref[...] = act
    spread(parts, jnp.dot(act, w_out_ref[...], preferred_element_type=F32), flip_ref, start)


def backward_kernel(count, start, flip_ref, *refs):
    blocks, (act_ref, w_in_ref, w_out_ref) = refs[:count], refs[count : count + 3]
    d_act = turned_dot(stack(blocks), w_out_ref[...])
    d_pre = jnp.where(act_ref[...] > 0, d_act, 0.0).astype(BF)
    terms = turned_dot(d_pre, w_in_ref[...])
    spread(refs[count + 3 :], terms, flip_ref, start)


def call(kernel, outs, scalars, *arrays, flops=0, limit=VMEM_LIMIT):
    vmem = pl.BlockSpec(memory_space=pltpu.VMEM)
    return pl.pallas_call(
        kernel,
        out_shape=outs,
        in_specs=[pl.BlockSpec(memory_space=pltpu.SMEM)] * scalars + [vmem] * (len(arrays) - scalars),
        out_specs=jax.tree.map(lambda _: vmem, outs),
        compiler_params=pltpu.CompilerParams(vmem_limit_bytes=limit),
        cost_estimate=pl.CostEstimate(flops=flops, bytes_accessed=2**20, transcendentals=0),
    )(*arrays)


def per_device(hidden, routes, gates, lengths, w_in, w_out, incoming):
    section = lax.axis_index("section")
    source, w_in, w_out = hidden[0], w_in[0], w_out[0]
    count, width = source.shape
    wide = jax.ShapeDtypeStruct((count, width), BF)
    slots = jax.ShapeDtypeStruct((SLOTS, width), BF)
    twice = jax.ShapeDtypeStruct((2 * SLOTS, width), BF)
    table = jax.ShapeDtypeStruct((SLOTS, count), BF)
    section_id = jnp.reshape(section.astype(jnp.int32), (1,))

    keep = jnp.where(section == 0, incoming[0], incoming[1])
    send = jnp.where(section == 0, incoming[1], incoming[0])

    rows, first, second = call(
        dispatch_kernel, [twice, table, table], 2, lengths, section_id, routes[0].T, source
    )

    hidden_units = w_in.shape[1]
    plane = lax.axis_index("expert") % SPLIT
    flips = jnp.stack([(plane + d) % SPLIT // (SPLIT // 2) for d in (0, -1, 1)]).astype(jnp.int32)
    acts = {}

    def run(kernel, key, blocks, extra, outs):
        start = (0, 1, None)[key]
        total = sum(b.shape[0] for b in blocks)
        outs = outs + [slots] * (total // SLOTS)
        got = call(
            functools.partial(kernel, len(blocks), start),
            outs,
            1,
            flips,
            *blocks,
            *extra,
            flops=COST * total * width * hidden_units,
        )
        terms = got[len(outs) - total // SLOTS :]
        return got, terms if start is None else list(zip(terms[::2], terms[1::2]))

    def forward(key, blocks):
        total = sum(b.shape[0] for b in blocks)
        outs = [jax.ShapeDtypeStruct((total, hidden_units), BF)]
        got, terms = run(forward_kernel, key, blocks, [w_in, w_out], outs)
        acts[key] = got[0]
        return terms

    def backward(key, blocks):
        return run(backward_kernel, key, blocks, [acts[key], w_in, w_out], [])[1]

    y, (keep, send) = exchange(rows, flips, forward, (keep, send))
    other = lax.ppermute(send, "section", [(0, 1), (1, 0)])
    y = swap_plane(y)

    result, upstream, gate_grad, grad_rows = call(
        middle_kernel,
        [wide, wide, jax.ShapeDtypeStruct((2, count), F32), twice],
        2,
        lengths,
        section_id,
        source,
        gates[0].T,
        first,
        second,
        y,
        keep,
        other,
    )

    d_rows = swap_plane(exchange(grad_rows, flips, backward)[0])

    hidden_grad = call(final_kernel, wide, 0, source, upstream, first, second, d_rows)
    return (result[None], hidden_grad[None], gate_grad.T[None])


def solution(mesh):
    in_specs = (
        P("section", "expert", None),
        P("section", "expert", None),
        P("section", "expert", None),
        P("section", "expert"),
        P("section", None, "expert"),
        P("section", "expert", None),
        P(None, "expert", "section"),
    )
    out_specs = (
        P("section", "expert", None),
        P("section", "expert", None),
        P("section", "expert", None),
    )
    return jax.shard_map(
        per_device, mesh=mesh, in_specs=in_specs, out_specs=out_specs, check_vma=False
    )
```

```python
import functools

import jax
import jax.numpy as jnp
from jax import lax
from jax.experimental import pallas as pl
from jax.experimental.pallas import tpu as pltpu
from jax.sharding import PartitionSpec as P

SPLIT = 8
CAP = 4
LIVE = 16
SLOTS = LIVE * CAP
EPS = 1e-05
COST = 1
BF = jnp.bfloat16
F32 = jnp.float32
VMEM_LIMIT = 16 * 2**20


def hop(value, step):
    n = lax.axis_size("expert")
    pairs = []
    for i in range(n):
        column = i // SPLIT * SPLIT
        pairs.append((i, column + (i + step) % SPLIT))
        pairs.append((n + i, n + column + (i - step) % SPLIT))
    return lax.ppermute(value, ("section", "expert"), pairs)


def swap_plane(rows):
    n = lax.axis_size("expert")
    groups = [[c * SPLIT + p for c in range(n // SPLIT)] for p in range(SPLIT)]
    count, width = rows.shape
    lanes = 128
    packed = rows.reshape(n // SPLIT, count * SPLIT // n * width // lanes, lanes)
    moved = lax.all_to_all(
        packed, "expert", split_axis=0, concat_axis=0, axis_index_groups=groups, tiled=True
    )
    return moved.reshape(count, width)


def swap_pair(rows):
    n = lax.axis_size("expert")
    half = SPLIT // 2
    groups = [[c * SPLIT + q for q in (p, p + half) for c in range(n // SPLIT)] for p in range(half)]
    count, width = rows.shape
    lanes = 128
    packed = rows.reshape(len(groups[0]), count * width // lanes // len(groups[0]), lanes)
    moved = lax.all_to_all(
        packed, "expert", split_axis=0, concat_axis=0, axis_index_groups=groups, tiled=True
    )
    return moved.reshape(count, width)


def nearer(pair, flip):
    half = pair.shape[0] // 2
    return jnp.where(flip, pair[half:], pair[:half])


def exchange(rows, flips, expert, ahead=()):
    pair = swap_pair(rows)
    up, down = hop(pair, 1), hop(pair, -1)
    if ahead:
        up, *ahead = lax.optimization_barrier((up, *ahead))
    ((own, across),) = expert(0, [pair])
    sum_up = hop(across, 1)
    up_2, down_2 = hop(nearer(up, flips[1] == 1), 1), hop(nearer(down, flips[2] == 1), -1)
    (low_1, high_3), (high_1, low_3) = expert(1, [up, down])
    sum_up, sum_down = hop(plus(sum_up, high_3), 1), hop(low_3, -1)
    low_2, high_2 = expert(2, [up_2, down_2])
    sum_up, sum_down = hop(plus(sum_up, high_2), 1), hop(plus(sum_down, low_2), -1)
    sum_up, sum_down = hop(plus(sum_up, high_1), 1), hop(plus(sum_down, low_1), -1)
    total = own.astype(F32) + sum_up.astype(F32) + sum_down.astype(F32)
    return total.astype(BF), ahead


def plus(a, b):
    return (a.astype(F32) + b.astype(F32)).astype(BF)


def normalize(values):
    center = values - jnp.mean(values, axis=-1, keepdims=True)
    scale = lax.rsqrt(jnp.mean(center * center, axis=-1, keepdims=True) + EPS)
    return center * scale, scale


def norm_back(normed, scale, upstream):
    first = jnp.mean(upstream, axis=-1, keepdims=True)
    second = jnp.mean(upstream * normed, axis=-1, keepdims=True)
    return scale * (upstream - first - normed * second)


def rows_dot(a, b):
    return lax.dot_general(a, b, (((0,), (0,)), ((), ())), preferred_element_type=F32)


def column(row):
    return jnp.broadcast_to(row, (row.shape[1], row.shape[1])).T[:, 0:1]


def row(column):
    return jnp.broadcast_to(column, (column.shape[0], column.shape[0])).T[0:1, :]


def dispatch_kernel(length_ref, section_ref, routes_ref, hidden_ref, rows_ref, first_ref, second_ref):
    count = hidden_ref.shape[0]
    slot = lax.broadcasted_iota(jnp.int32, (SLOTS, count), 0)
    token = lax.broadcasted_iota(jnp.int32, (SLOTS, count), 1)
    expert, place = slot // CAP, slot % CAP
    alive = token < length_ref[0, 0]
    hit0 = alive & (routes_ref[0:1, :] == expert)
    hit1 = alive & (routes_ref[1:2, :] == expert)
    hits = jnp.where(hit0 | hit1, 1.0, 0.0).astype(BF)
    earlier = lax.broadcasted_iota(jnp.int32, (count, count), 0) < lax.broadcasted_iota(
        jnp.int32, (count, count), 1
    )
    rank = jnp.dot(hits, jnp.where(earlier, 1.0, 0.0).astype(BF), preferred_element_type=F32)
    here = rank == place.astype(F32)
    first = jnp.where(hit0 & here, 1.0, 0.0).astype(BF)
    second = jnp.where(hit1 & here, 1.0, 0.0).astype(BF)
    first_ref[...] = first
    second_ref[...] = second
    normed, _ = normalize(hidden_ref[...].astype(F32))
    rows = jnp.dot(first + second, normed.astype(BF), preferred_element_type=F32).astype(BF)
    rows_ref[:SLOTS] = rows
    rows_ref[SLOTS:] = rows


def middle_kernel(
    length_ref,
    section_ref,
    hidden_ref,
    gates_ref,
    first_ref,
    second_ref,
    y_ref,
    keep_ref,
    other_ref,
    result_ref,
    upstream_ref,
    gate_grad_ref,
    rows_ref,
):
    count = hidden_ref.shape[0]
    encoder = section_ref[0] == 0
    alive = lax.broadcasted_iota(jnp.int32, (count, 1), 0) < length_ref[0, 0]
    g0, g1 = column(gates_ref[0:1, :]), column(gates_ref[1:2, :])
    y = y_ref[...]
    y0 = rows_dot(first_ref[...], y)
    y1 = rows_dot(second_ref[...], y)
    layer_out = (hidden_ref[...].astype(F32) + g0 * y0 + g1 * y1).astype(BF)
    hat, scale = normalize(layer_out.astype(F32))
    result_ref[...] = jnp.where(encoder, hat.astype(BF), layer_out)
    keep, other = keep_ref[...].astype(F32), other_ref[...].astype(F32)
    cot = jnp.concatenate(
        [jnp.where(encoder, keep, other), jnp.where(encoder, other, keep)], axis=1
    )
    cot = jnp.where(alive, cot, 0.0)
    upstream = jnp.where(encoder, norm_back(hat, scale, cot), cot).astype(BF)
    upstream_ref[...] = upstream
    up32 = upstream.astype(F32)
    gate_grad_ref[0:1, :] = row(jnp.sum(up32 * y0, axis=-1, keepdims=True))
    gate_grad_ref[1:2, :] = row(jnp.sum(up32 * y1, axis=-1, keepdims=True))
    rows = jnp.dot(first_ref[...], (g0 * up32).astype(BF), preferred_element_type=F32)
    rows += jnp.dot(second_ref[...], (g1 * up32).astype(BF), preferred_element_type=F32)
    rows_ref[:SLOTS] = rows.astype(BF)
    rows_ref[SLOTS:] = rows.astype(BF)


def final_kernel(hidden_ref, upstream_ref, first_ref, second_ref, d_ref, out_ref):
    normed, scale = normalize(hidden_ref[...].astype(F32))
    d_normed = rows_dot(first_ref[...] + second_ref[...], d_ref[...])
    out_ref[...] = (upstream_ref[...].astype(F32) + norm_back(normed, scale, d_normed)).astype(BF)


def turned_dot(a, b):
    return lax.dot_general(a, b, (((1,), (1,)), ((), ())), preferred_element_type=F32)


def stack(refs):
    return jnp.concatenate([ref[...] for ref in refs], axis=0) if len(refs) > 1 else refs[0][...]


def spread(refs, terms, flip_ref, start):
    rows = refs[0].shape[0]
    for i in range(0, len(refs), 1 if start is None else 2):
        part = terms[i * rows : (i + 1) * rows]
        if start is None:
            refs[i][...] = part.astype(BF)
            continue
        other = terms[(i + 1) * rows : (i + 2) * rows]
        flip = flip_ref[start + i // 2] == 1
        refs[i][...] = jnp.where(flip, other, part).astype(BF)
        refs[i + 1][...] = jnp.where(flip, part, other).astype(BF)


def forward_kernel(count, start, flip_ref, *refs):
    blocks, (w_in_ref, w_out_ref) = refs[:count], refs[count : count + 2]
    act_ref, parts = refs[count + 2], refs[count + 3 :]
    act = jnp.dot(stack(blocks), w_in_ref[...], preferred_element_type=F32)
    act = jnp.maximum(act, 0.0).astype(BF)
    act_ref[...] = act
    spread(parts, jnp.dot(act, w_out_ref[...], preferred_element_type=F32), flip_ref, start)


def backward_kernel(count, start, flip_ref, *refs):
    blocks, (act_ref, w_in_ref, w_out_ref) = refs[:count], refs[count : count + 3]
    d_act = turned_dot(stack(blocks), w_out_ref[...])
    d_pre = jnp.where(act_ref[...] > 0, d_act, 0.0).astype(BF)
    terms = turned_dot(d_pre, w_in_ref[...])
    spread(refs[count + 3 :], terms, flip_ref, start)


def call(kernel, outs, scalars, *arrays, flops=0, limit=VMEM_LIMIT):
    vmem = pl.BlockSpec(memory_space=pltpu.VMEM)
    return pl.pallas_call(
        kernel,
        out_shape=outs,
        in_specs=[pl.BlockSpec(memory_space=pltpu.SMEM)] * scalars + [vmem] * (len(arrays) - scalars),
        out_specs=jax.tree.map(lambda _: vmem, outs),
        compiler_params=pltpu.CompilerParams(vmem_limit_bytes=limit),
        cost_estimate=pl.CostEstimate(flops=flops, bytes_accessed=2**20, transcendentals=0),
    )(*arrays)


def per_device(hidden, routes, gates, lengths, w_in, w_out, incoming):
    section = lax.axis_index("section")
    source, w_in, w_out = hidden[0], w_in[0], w_out[0]
    count, width = source.shape
    wide = jax.ShapeDtypeStruct((count, width), BF)
    slots = jax.ShapeDtypeStruct((SLOTS, width), BF)
    twice = jax.ShapeDtypeStruct((2 * SLOTS, width), BF)
    table = jax.ShapeDtypeStruct((SLOTS, count), BF)
    section_id = jnp.reshape(section.astype(jnp.int32), (1,))

    keep = jnp.where(section == 0, incoming[0], incoming[1])
    send = jnp.where(section == 0, incoming[1], incoming[0])

    rows, first, second = call(
        dispatch_kernel, [twice, table, table], 2, lengths, section_id, routes[0].T, source
    )

    hidden_units = w_in.shape[1]
    plane = lax.axis_index("expert") % SPLIT
    turn = jnp.where(section == 0, 1, -1)
    flips = jnp.stack([(plane + d * turn) % SPLIT // (SPLIT // 2) for d in (0, -1, 1)])
    flips = flips.astype(jnp.int32)
    acts = {}

    def run(kernel, key, blocks, extra, outs):
        start = (0, 1, None)[key]
        total = sum(b.shape[0] for b in blocks)
        outs = outs + [slots] * (total // SLOTS)
        got = call(
            functools.partial(kernel, len(blocks), start),
            outs,
            1,
            flips,
            *blocks,
            *extra,
            flops=COST * total * width * hidden_units,
        )
        terms = got[len(outs) - total // SLOTS :]
        return got, terms if start is None else list(zip(terms[::2], terms[1::2]))

    def forward(key, blocks):
        total = sum(b.shape[0] for b in blocks)
        outs = [jax.ShapeDtypeStruct((total, hidden_units), BF)]
        got, terms = run(forward_kernel, key, blocks, [w_in, w_out], outs)
        acts[key] = got[0]
        return terms

    def backward(key, blocks):
        return run(backward_kernel, key, blocks, [acts[key], w_in, w_out], [])[1]

    y, (keep, send) = exchange(rows, flips, forward, (keep, send))
    other = lax.ppermute(send, "section", [(0, 1), (1, 0)])
    y = swap_plane(y)

    result, upstream, gate_grad, grad_rows = call(
        middle_kernel,
        [wide, wide, jax.ShapeDtypeStruct((2, count), F32), twice],
        2,
        lengths,
        section_id,
        source,
        gates[0].T,
        first,
        second,
        y,
        keep,
        other,
    )

    d_rows = swap_plane(exchange(grad_rows, flips, backward)[0])

    hidden_grad = call(final_kernel, wide, 0, source, upstream, first, second, d_rows)
    return (result[None], hidden_grad[None], gate_grad.T[None])


def solution(mesh):
    in_specs = (
        P("section", "expert", None),
        P("section", "expert", None),
        P("section", "expert", None),
        P("section", "expert"),
        P("section", None, "expert"),
        P("section", "expert", None),
        P(None, "expert", "section"),
    )
    out_specs = (
        P("section", "expert", None),
        P("section", "expert", None),
        P("section", "expert", None),
    )
    return jax.shard_map(
        per_device, mesh=mesh, in_specs=in_specs, out_specs=out_specs, check_vma=False
    )
```
